128 devices in a mesh: blk: 16 (over x_lo, y, core), grp: 8 (over z, x_hi).
Axes of the slice: x: 4 (x_hi: 2, x_lo: 2; x = x_hi * 2 + x_lo), y: 4, z: 4, core: 2. Of those that a mesh axis runs over, the one named last changes fastest.
Arguments:
- picture_vectors: bfloat16 [16384, 1152], P(('blk', 'grp')), may hold values from -6 to 6
- caption_vectors: bfloat16 [16384, 1152], P(('blk', 'grp')), may hold values from -6 to 6
- ln_inverse_warmth: float32 [], replicated, may hold values from 1.6 to 2.7
- score_offset: float32 [], replicated, may hold values from -2 to 0
- objective_multiplier: float32 [], replicated, may hold values from 32768 to 262144
Outputs:
- image_grad: bfloat16 [16384, 1152], P(('blk', 'grp'))
- text_grad: bfloat16 [16384, 1152], P(('blk', 'grp'))
The draws below stay inside these ranges and needn't reach their ends.
All inputs are finite; a program needn't handle non-finite values.
Results may differ from the reference program's by a relative error of at most 0.017.
Values may be sent and summed in bfloat16 or wider, within the bound.
No kernel may reach another device: no remote copies, remote signals or barrier semaphores. Data moves between devices by JAX's collectives and lax.ppermute only.
A program may use at most 64 MiB of HBM per device.

```python
import math
import jax
import jax.numpy as jnp
from jax import lax

D = 1152
GROUP_ROWS = 1024
BATCH = 16384


def block_scale(stream_key, extent, split, low, largest):
    factor_of, own = 1.0, jax.random.fold_in(stream_key, 6)
    for axis_at, shards_of in split:
        steps = jnp.exp(jax.random.uniform(jax.random.fold_in(own, axis_at), (shards_of,), jnp.float32, low / len(split), largest / len(split)))
        factor_of = factor_of * jnp.repeat(steps, extent[axis_at] // shards_of).reshape([-1 if axis == axis_at else 1 for axis in range(len(extent))])
    return factor_of


def scatter_about(rng, dims, width, most, pieces=(), held_as=jnp.bfloat16):
    array = jax.random.normal(rng, dims, jnp.float32) * width
    if len(pieces) > 0:
        array = block_scale(rng, dims, pieces, -0.22, 0.18) * array
    return jnp.clip(array, min=-most, max=most).astype(held_as)


def setup_inputs(seed: int = 0) -> dict:
    streams_of = jax.random.split(jax.random.key(seed), 6)
    return {
        "picture_vectors": scatter_about(streams_of[0], (BATCH, D), 1.0, 6.0, ((0, 128),)),
        "caption_vectors": scatter_about(streams_of[1], (BATCH, D), 1.0, 6.0, ((0, 128),)),
        "ln_inverse_warmth": jnp.clip(jax.random.uniform(streams_of[2], (), jnp.float32, 1.6, 2.7), 1.6, 2.7),
        "score_offset": jnp.clip(jax.random.uniform(streams_of[3], (), jnp.float32, -2.0, 0.0), -2.0, 0.0),
        "objective_multiplier": jnp.clip(jnp.exp(jax.random.uniform(streams_of[4], (), jnp.float32, math.log(32768.0), math.log(262144.0))), 32768.0, 262144.0),
    }


def unit_rows(raw):
    values = raw.astype(jnp.float32)
    inverse = lax.rsqrt(lax.optimization_barrier(jnp.sum(values * values, axis=1, keepdims=True)) + 1e-06)
    return (values * inverse, inverse)

def through_norm(unit, inverse, direct):
    along = lax.optimization_barrier(jnp.sum(unit * direct, axis=1, keepdims=True))
    return (inverse * (direct - unit * along)).astype(jnp.bfloat16)

def reference(picture_vectors, caption_vectors, ln_inverse_warmth, score_offset, objective_multiplier):
    image_unit, image_inv = unit_rows(picture_vectors)
    text_unit, text_inv = unit_rows(caption_vectors)
    image_half = image_unit.astype(jnp.bfloat16)
    caption_subset_entries = text_unit.astype(jnp.bfloat16)
    score_multiplier = jnp.exp(ln_inverse_warmth)
    sigmoid_coefficient = objective_multiplier / BATCH
    column_ids = jnp.arange(BATCH, dtype=jnp.int32)
    row_local = jnp.arange(GROUP_ROWS, dtype=jnp.int32)

    def visit(text_total, block_index):
        start = (block_index * GROUP_ROWS).astype(jnp.int32)
        picture_entry_range = lax.dynamic_slice_in_dim(image_half, start, GROUP_ROWS, 0)
        similarity_scores = score_multiplier * lax.dot_general(picture_entry_range, caption_subset_entries, (((1,), (1,)), ((), ())), preferred_element_type=jnp.float32) + score_offset
        match = (start + row_local)[:, None] == column_ids[None, :]
        match_polarity = jnp.where(match, jnp.float32(1.0), jnp.float32(-1.0))
        score_derivative = (-(sigmoid_coefficient * score_multiplier) * match_polarity * jax.nn.sigmoid(-match_polarity * similarity_scores)).astype(jnp.bfloat16)
        image_dir = jnp.dot(score_derivative, caption_subset_entries, preferred_element_type=jnp.float32)
        text_part = lax.dot_general(score_derivative, picture_entry_range, (((0,), (0,)), ((), ())), preferred_element_type=jnp.float32)
        text_round = lax.optimization_barrier(text_part.astype(jnp.bfloat16))
        return (text_total + text_round.astype(jnp.float32), image_dir)
    blocks = jnp.arange(BATCH // GROUP_ROWS, dtype=jnp.int32)
    text_dir, image_parts = lax.scan(visit, jnp.zeros((BATCH, D), jnp.float32), blocks)
    image_dir = image_parts.reshape(BATCH, D)
    return (through_norm(image_unit, image_inv, image_dir), through_norm(text_unit, text_inv, text_dir))
```

```python
from functools import partial

import jax
import jax.numpy as jnp
from jax import lax
from jax.experimental import pallas as pl
from jax.experimental.pallas import tpu as pltpu
from jax.sharding import PartitionSpec as P

RING = 4
CORES = 2
TILE = 256
COPY_ROWS = 32
VMEM_BYTES = 24 * 1024 * 1024


def place(x, y, z, core):
    blk = ((x % 2) * RING + y) * CORES + core
    return blk * 8 + z * 2 + x // 2


def sender(move):
    pairs = [
        (place(x, y, z, core), place(*move(x, y, z, core)))
        for x in range(RING)
        for y in range(RING)
        for z in range(RING)
        for core in range(CORES)
    ]
    return lambda value: lax.ppermute(value, ("blk", "grp"), pairs)


def ring(steps):
    return sender(
        lambda x, y, z, c: (x, y, (z + steps) % RING, c) if c else (x, (y + steps) % RING, z, c)
    )


to_core = sender(lambda x, y, z, c: (x, y, z, 1 - c))
cross = sender(lambda x, y, z, c: (3 - x if c else x ^ 1, y, z, c))
up, down = ring(1), ring(RING - 1)


def call(name, body, out_shape, operands, flops, scalars=(), after=(), scratch=()):
    moved = sum(2 * value.size for value in operands) + sum(2 * shape.size for shape in out_shape)
    out = pl.pallas_call(
        lambda *refs: body(*refs[len(after) :]),
        name=name,
        out_shape=out_shape,
        in_specs=[pl.BlockSpec(memory_space=pl.ANY)] * len(after)
        + [pl.BlockSpec(memory_space=pltpu.SMEM)] * len(scalars)
        + [pl.BlockSpec(memory_space=pltpu.VMEM)] * len(operands),
        scratch_shapes=list(scratch),
        compiler_params=pltpu.CompilerParams(vmem_limit_bytes=VMEM_BYTES),
        cost_estimate=pl.CostEstimate(flops=flops // 64, bytes_accessed=moved // 64, transcendentals=0),
    )(*after, *scalars, *operands)
    return list(out)


def array(rows, columns):
    return jax.ShapeDtypeStruct((rows, columns), jnp.bfloat16)


def total_of(terms):
    total = terms[0].astype(jnp.float32)
    for term in terms[1:]:
        total = total + term.astype(jnp.float32)
    return total


def add(*terms, flops=0, after=()):
    def body(*refs):
        refs[-1][...] = total_of([ref[...] for ref in refs[:-1]]).astype(jnp.bfloat16)

    return call("add", body, [array(*terms[0].shape)], terms, flops, after=after)[0]


def unit_of(values):
    inverse = lax.rsqrt(jnp.sum(values * values, axis=1, keepdims=True) + 1e-06)
    return values * inverse, inverse


def unit_halves(core, parameters, batch_total, picture, caption):
    def body(core, warmth, score_offset, multiplier, picture_ref, caption_ref, *refs):
        keep, give, constants, image, text, sems = refs
        copies = []
        for source, target in ((picture_ref, image), (caption_ref, text)):
            for first in range(0, source.shape[0], COPY_ROWS):
                here = pl.ds(first, COPY_ROWS)
                copies.append(
                    pltpu.make_async_copy(
                        source.at[here, :], target.at[here, :], sems.at[len(copies)]
                    )
                )
        for copy in copies:
            copy.start()
        scale = jnp.exp(jnp.full((1, TILE), warmth[0], jnp.float32))
        constants[0:1, :] = 0.5 * scale
        constants[1:2, :] = jnp.full((1, TILE), 0.5 * score_offset[0], jnp.float32)
        constants[2:3, :] = 0.5 * (multiplier[0] / batch_total * scale)
        for copy in copies:
            copy.wait()

        @pl.when(core[0] == 0)
        def _():
            give[...] = unit_of(image[...].astype(jnp.float32))[0].astype(jnp.bfloat16)
            keep[...] = unit_of(text[...].astype(jnp.float32))[0].astype(jnp.bfloat16)

        @pl.when(core[0] != 0)
        def _():
            give[...] = unit_of(text[...].astype(jnp.float32))[0].astype(jnp.bfloat16)
            keep[...] = unit_of(image[...].astype(jnp.float32))[0].astype(jnp.bfloat16)

    return pl.pallas_call(
        body,
        name="units",
        out_shape=[array(*picture.shape)] * 2 + [jax.ShapeDtypeStruct((8, TILE), jnp.float32)],
        in_specs=[pl.BlockSpec(memory_space=pltpu.SMEM)] * 4
        + [pl.BlockSpec(memory_space=pltpu.HBM)] * 2,
        scratch_shapes=[
            pltpu.VMEM(picture.shape, jnp.bfloat16),
            pltpu.VMEM(picture.shape, jnp.bfloat16),
            pltpu.SemaphoreType.DMA((2 * picture.shape[0] // COPY_ROWS,)),
        ],
        compiler_params=pltpu.CompilerParams(vmem_limit_bytes=VMEM_BYTES),
    )(core, *parameters, picture, caption)


def pack(*blocks):
    rows, feature = blocks[0].shape

    def body(*refs):
        for at, ref in enumerate(refs[:-1]):
            refs[-1][pl.ds(at * rows, rows), :] = ref[...]

    return call("pack", body, [array(len(blocks) * rows, feature)], blocks, rows * feature)[0]


def stacked(refs):
    return jnp.concatenate([ref[...] for ref in refs], axis=0)


def sums(name, constants, left, right, held=None, own=False, rows_out=None, after=()):
    feature = left[0].shape[1]
    count, others = sum(ref.shape[0] for ref in left), sum(ref.shape[0] for ref in right)
    blocks = 1 if rows_out is None else count // rows_out

    def body(constants, *refs):
        left_refs, right_refs = refs[: len(left)], refs[len(left) :][: len(right)]
        refs = refs[len(left) + len(right) :]
        out, grads = refs[-1 - blocks : -1], refs[-1]
        slope, shift, factor = constants[0:1, :], constants[1:2, :], constants[2:3, :]
        tiles = [
            (ref, first)
            for ref, block in zip(right_refs, right)
            for first in range(0, block.shape[0], TILE)
        ]

        def scores(tile):
            ref, first = tile
            return lax.dot_general(
                stacked(left_refs),
                ref[pl.ds(first, TILE), :],
                (((1,), (1,)), ((), ())),
                preferred_element_type=jnp.float32,
            )

        upcoming = scores(tiles[0])
        for index in range(len(tiles)):
            current = upcoming
            if index + 1 < len(tiles):
                upcoming = scores(tiles[index + 1])
            bent = jnp.tanh(current * slope + shift) * factor
            offset = factor
            if own and index == 0:
                row = lax.broadcasted_iota(jnp.int32, bent.shape, 0)
                column = lax.broadcasted_iota(jnp.int32, bent.shape, 1)
                half = TILE // 2
                partner = jnp.where(row < half, row + half, row - half)
                paired = jnp.logical_and(column == partner, row < TILE)
                offset = jnp.where(paired, -factor, factor)
            grads[:, pl.ds(index * TILE, TILE)] = (bent + offset).astype(jnp.bfloat16)
        total = jnp.dot(grads[...], stacked(right_refs), preferred_element_type=jnp.float32)
        if held is not None:
            total = total + refs[0][...]
        if rows_out is None:
            out[0][...] = total
        else:
            for at, ref in enumerate(out):
                ref[...] = total[at * rows_out : (at + 1) * rows_out].astype(jnp.bfloat16)

    shapes = (
        [jax.ShapeDtypeStruct((count, feature), jnp.float32)]
        if rows_out is None
        else [array(rows_out, feature)] * blocks
    )
    return call(
        name,
        body,
        shapes,
        [constants, *left, *right] + ([] if held is None else [held]),
        4 * count * others * feature,
        (),
        after,
        [pltpu.VMEM((count, others), jnp.bfloat16)],
    )


def add_half(whole, part, half, flops=0, after=()):
    rows = part.shape[0]

    def body(whole, part, out):
        out[pl.ds((1 - half) * rows, rows), :] = whole[pl.ds((1 - half) * rows, rows), :]
        here = pl.ds(half * rows, rows)
        out[here, :] = total_of([whole[here, :], part[...]]).astype(jnp.bfloat16)

    return call("add_half", body, [array(*whole.shape)], [whole, part], flops, after=after)[0]


def through_norms(core, picture, caption, terms):
    rows, feature = picture.shape

    def give_body(*refs):
        total = total_of([ref[pl.ds(rows, rows), :] for ref in refs[:-1]])
        refs[-1][...] = total.astype(jnp.bfloat16)

    got = to_core(call("give", give_body, [array(rows, feature)], terms, 4 * rows * feature)[0])

    def body(core, picture, caption, got, *refs):
        kept, (image_out, text_out) = refs[:-2], refs[-2:]

        def finish(raw, direct, out):
            unit, inverse = unit_of(raw[...].astype(jnp.float32))
            along = jnp.sum(unit * direct, axis=1, keepdims=True)
            out[...] = (inverse * (direct - unit * along)).astype(jnp.bfloat16)

        def direct_kept():
            return total_of([ref[pl.ds(0, rows), :] for ref in kept])

        @pl.when(core[0] == 0)
        def _():
            finish(picture, got[...].astype(jnp.float32), image_out)
            finish(caption, direct_kept(), text_out)

        @pl.when(core[0] != 0)
        def _():
            finish(picture, direct_kept(), image_out)
            finish(caption, got[...].astype(jnp.float32), text_out)

    return call(
        "final",
        body,
        [array(rows, feature)] * 2,
        [picture, caption, got, *terms],
        20 * rows * feature,
        [core],
    )


def on_device(
    picture_vectors, caption_vectors, ln_inverse_warmth, score_offset, objective_multiplier
):
    batch_total = picture_vectors.shape[0] * lax.axis_size(("blk", "grp"))
    parameters = [
        value.reshape(1) for value in (ln_inverse_warmth, score_offset, objective_multiplier)
    ]
    core = (lax.axis_index("blk") & (CORES - 1)).reshape(1)
    rows = picture_vectors.shape[0]
    keep, give, constants = unit_halves(
        core, parameters, batch_total, picture_vectors, caption_vectors
    )
    own = jnp.concatenate([keep, to_core(give)], axis=0)
    partner, below, above = cross(own), up(own), down(own)
    partner_above, partner_below, far = cross(above), up(partner), down(above)
    near = [own, partner, above, below]
    near_other = [to_core(block) for block in near]
    near_held = sums("near", constants, near, near_other, own=True)[0]
    partner_below, near_held = lax.optimization_barrier((partner_below, near_held))
    far, near_held = lax.optimization_barrier((far, near_held))
    last = cross(far[:rows]), up(partner_below[rows:])
    middle = [partner_above, partner_below, far]
    middle_other = [to_core(block) for block in middle]
    middle_held = sums("middle", constants, middle, near_other)[0]
    *last, middle_held = lax.optimization_barrier((*last, middle_held))
    last = pack(*last)
    last_other = to_core(last)
    last_held = sums("last", constants, [last], [*near_other, *middle_other])[0]

    last_0, last_1 = sums("last_rest", constants, [last], [last_other], last_held, rows_out=rows)
    to_far, to_below = cross(last_0), down(last_1)
    rest = [*middle_other, last_other]
    partner_above, partner_below, far = sums(
        "middle_rest", constants, middle, rest, middle_held, rows_out=2 * rows, after=[last_0]
    )
    far, partner_below = add_half(far, to_far, 0), add_half(partner_below, to_below, 1)
    to_above, to_partner, to_above_too = up(far), down(partner_below), cross(partner_above)
    own, partner, above, below = sums(
        "near_rest",
        constants,
        near,
        rest,
        near_held,
        rows_out=2 * rows,
        after=[far, partner_below],
    )
    above, partner = add(above, to_above, to_above_too), add(partner, to_partner)
    terms = [own, up(above), down(below), cross(partner)]
    image_grad, text_grad = through_norms(core, picture_vectors, caption_vectors, terms)
    return image_grad, text_grad


def solution(mesh):
    return jax.shard_map(
        on_device,
        mesh=mesh,
        in_specs=(P(("blk", "grp"), None), P(("blk", "grp"), None), P(), P(), P()),
        out_specs=(P(("blk", "grp"), None), P(("blk", "grp"), None)),
        check_vma=False,
    )
```

```python
from functools import partial

import jax
import jax.numpy as jnp
from jax import lax
from jax.experimental import pallas as pl
from jax.experimental.pallas import tpu as pltpu
from jax.sharding import PartitionSpec as P

RING = 4
CORES = 2
TILE = 256
VMEM_BYTES = 24 * 1024 * 1024


def place(x, y, z, core):
    blk = ((x % 2) * RING + y) * CORES + core
    return blk * 8 + z * 2 + x // 2


def sender(move):
    pairs = [
        (place(x, y, z, core), place(*move(x, y, z, core)))
        for x in range(RING)
        for y in range(RING)
        for z in range(RING)
        for core in range(CORES)
    ]
    return lambda value: lax.ppermute(value, ("blk", "grp"), pairs)


def sender_pair(move):
    return sender(move), sender(lambda *at: (*move(*at)[:3], 1 - at[3]))


def ring(steps):
    return sender_pair(
        lambda x, y, z, c: (x, y, (z + steps) % RING, c) if c else (x, (y + steps) % RING, z, c)
    )


to_core = sender(lambda x, y, z, c: (x, y, z, 1 - c))
cross, cross_over = sender_pair(lambda x, y, z, c: (3 - x if c else x ^ 1, y, z, c))
(up, up_over), (down, down_over) = ring(1), ring(RING - 1)


def call(name, body, out_shape, operands, flops, scalars=(), after=(), scratch=()):
    moved = sum(2 * value.size for value in operands) + sum(2 * shape.size for shape in out_shape)
    out = pl.pallas_call(
        lambda *refs: body(*refs[len(after) :]),
        name=name,
        out_shape=out_shape,
        in_specs=[pl.BlockSpec(memory_space=pl.ANY)] * len(after)
        + [pl.BlockSpec(memory_space=pltpu.SMEM)] * len(scalars)
        + [pl.BlockSpec(memory_space=pltpu.VMEM)] * len(operands),
        scratch_shapes=list(scratch),
        compiler_params=pltpu.CompilerParams(vmem_limit_bytes=VMEM_BYTES),
        cost_estimate=pl.CostEstimate(flops=flops // 64, bytes_accessed=moved // 64, transcendentals=0),
    )(*after, *scalars, *operands)
    return list(out)


def array(rows, columns):
    return jax.ShapeDtypeStruct((rows, columns), jnp.bfloat16)


def total_of(terms):
    total = terms[0].astype(jnp.float32)
    for term in terms[1:]:
        total = total + term.astype(jnp.float32)
    return total


def add(*terms, flops=0, after=()):
    def body(*refs):
        refs[-1][...] = total_of([ref[...] for ref in refs[:-1]]).astype(jnp.bfloat16)

    return call("add", body, [array(*terms[0].shape)], terms, flops, after=after)[0]


def unit_of(values):
    inverse = lax.rsqrt(jnp.sum(values * values, axis=1, keepdims=True) + 1e-06)
    return values * inverse, inverse


def unit_halves(core, parameters, batch_total, picture, caption):
    def body(core, warmth, score_offset, multiplier, picture, caption, keep, give, constants):
        scale = jnp.exp(jnp.full((1, TILE), warmth[0], jnp.float32))
        constants[0:1, :] = 0.5 * scale
        constants[1:2, :] = jnp.full((1, TILE), 0.5 * score_offset[0], jnp.float32)
        constants[2:3, :] = 0.5 * (multiplier[0] / batch_total * scale)

        def fill(carried, handed):
            keep[...] = unit_of(carried[...].astype(jnp.float32))[0].astype(jnp.bfloat16)
            give[...] = unit_of(handed[...].astype(jnp.float32))[0].astype(jnp.bfloat16)

        @pl.when(core[0] == 0)
        def _():
            fill(caption, picture)

        @pl.when(core[0] != 0)
        def _():
            fill(picture, caption)

    shapes = [array(*picture.shape)] * 2 + [jax.ShapeDtypeStruct((8, TILE), jnp.float32)]
    return call("units", body, shapes, [picture, caption], 6 * picture.size, [core, *parameters])


def pack(*blocks):
    rows, feature = blocks[0].shape

    def body(*refs):
        for at, ref in enumerate(refs[:-1]):
            refs[-1][pl.ds(at * rows, rows), :] = ref[...]

    return call("pack", body, [array(len(blocks) * rows, feature)], blocks, rows * feature)[0]


def stacked(refs):
    return jnp.concatenate([ref[...] for ref in refs], axis=0)


def sums(name, constants, left, right, held=None, own=False, rows_out=None, after=()):
    feature = left[0].shape[1]
    count, others = sum(ref.shape[0] for ref in left), sum(ref.shape[0] for ref in right)
    blocks = 1 if rows_out is None else count // rows_out

    def body(constants, *refs):
        left_refs, right_refs = refs[: len(left)], refs[len(left) :][: len(right)]
        refs = refs[len(left) + len(right) :]
        out, grads = refs[-1 - blocks : -1], refs[-1]
        slope, shift, factor = constants[0:1, :], constants[1:2, :], constants[2:3, :]
        tiles = [
            (ref, first)
            for ref, block in zip(right_refs, right)
            for first in range(0, block.shape[0], TILE)
        ]

        def scores(tile):
            ref, first = tile
            return lax.dot_general(
                stacked(left_refs),
                ref[pl.ds(first, TILE), :],
                (((1,), (1,)), ((), ())),
                preferred_element_type=jnp.float32,
            )

        upcoming = scores(tiles[0])
        for index in range(len(tiles)):
            current = upcoming
            if index + 1 < len(tiles):
                upcoming = scores(tiles[index + 1])
            bent = jnp.tanh(current * slope + shift) * factor
            offset = factor
            if own and index == 0:
                row = lax.broadcasted_iota(jnp.int32, bent.shape, 0)
                column = lax.broadcasted_iota(jnp.int32, bent.shape, 1)
                half = TILE // 2
                partner = jnp.where(row < half, row + half, row - half)
                paired = jnp.logical_and(column == partner, row < TILE)
                offset = jnp.where(paired, -factor, factor)
            grads[:, pl.ds(index * TILE, TILE)] = (bent + offset).astype(jnp.bfloat16)
        total = jnp.dot(grads[...], stacked(right_refs), preferred_element_type=jnp.float32)
        if held is not None:
            total = total + refs[0][...]
        if rows_out is None:
            out[0][...] = total
        else:
            for at, ref in enumerate(out):
                ref[...] = total[at * rows_out : (at + 1) * rows_out].astype(jnp.bfloat16)

    shapes = (
        [jax.ShapeDtypeStruct((count, feature), jnp.float32)]
        if rows_out is None
        else [array(rows_out, feature)] * blocks
    )
    return call(
        name,
        body,
        shapes,
        [constants, *left, *right] + ([] if held is None else [held]),
        4 * count * others * feature,
        (),
        after,
        [pltpu.VMEM((count, others), jnp.bfloat16)],
    )


def add_half(whole, part, half, flops=0, after=()):
    rows = part.shape[0]

    def body(whole, part, out):
        out[pl.ds((1 - half) * rows, rows), :] = whole[pl.ds((1 - half) * rows, rows), :]
        here = pl.ds(half * rows, rows)
        out[here, :] = total_of([whole[here, :], part[...]]).astype(jnp.bfloat16)

    return call("add_half", body, [array(*whole.shape)], [whole, part], flops, after=after)[0]


def add_halves(halves, *terms):
    rows = halves[0].shape[0]

    def body(*refs):
        for half in range(2):
            parts = [refs[half][...]]
            parts += [ref[pl.ds(half * rows, rows), :] for ref in refs[2:-2]]
            refs[half - 2][...] = total_of(parts).astype(jnp.bfloat16)

    return call("add_halves", body, [array(*halves[0].shape)] * 2, [*halves, *terms], 0)


def through_norms(core, picture, caption, carried, handed):
    rows, feature = picture.shape
    count = len(carried)

    def body(core, picture, caption, *refs):
        carried, handed, (image_out, text_out) = refs[:count], refs[count:-2], refs[-2:]

        def finish(raw, terms, out):
            direct = total_of([ref[...] for ref in terms])
            unit, inverse = unit_of(raw[...].astype(jnp.float32))
            along = jnp.sum(unit * direct, axis=1, keepdims=True)
            out[...] = (inverse * (direct - unit * along)).astype(jnp.bfloat16)

        @pl.when(core[0] == 0)
        def _():
            finish(picture, handed, image_out)
            finish(caption, carried, text_out)

        @pl.when(core[0] != 0)
        def _():
            finish(picture, carried, image_out)
            finish(caption, handed, text_out)

    return call(
        "final",
        body,
        [array(rows, feature)] * 2,
        [picture, caption, *carried, *handed],
        20 * rows * feature,
        [core],
    )


def on_device(
    picture_vectors, caption_vectors, ln_inverse_warmth, score_offset, objective_multiplier
):
    batch_total = picture_vectors.shape[0] * lax.axis_size(("blk", "grp"))
    parameters = [
        value.reshape(1) for value in (ln_inverse_warmth, score_offset, objective_multiplier)
    ]
    core = (lax.axis_index("blk") & (CORES - 1)).reshape(1)
    rows = picture_vectors.shape[0]
    keep, give, constants = unit_halves(
        core, parameters, batch_total, picture_vectors, caption_vectors
    )
    own = jnp.concatenate([keep, to_core(give)], axis=0)
    partner, below, above = cross(own), up(own), down(own)
    partner_above, partner_below, far = cross(above), up(partner), down(above)
    near = [own, partner, above, below]
    near_other = [to_core(block) for block in near]
    near_held = sums("near", constants, near, near_other, own=True)[0]
    partner_below, near_held = lax.optimization_barrier((partner_below, near_held))
    far, near_held = lax.optimization_barrier((far, near_held))
    last = cross(far[:rows]), up(partner_below[rows:])
    middle = [partner_above, partner_below, far]
    middle_other = [to_core(block) for block in middle]
    middle_held = sums("middle", constants, middle, near_other)[0]
    *last, middle_held = lax.optimization_barrier((*last, middle_held))
    last = pack(*last)
    last_other = to_core(last)
    last_held = sums("last", constants, [last], [*near_other, *middle_other])[0]

    last_0, last_1 = sums("last_rest", constants, [last], [last_other], last_held, rows_out=rows)
    to_far, to_below = cross(last_0), down(last_1)
    rest = [*middle_other, last_other]
    partner_above, partner_below, far = sums(
        "middle_rest", constants, middle, rest, middle_held, rows_out=2 * rows, after=[last_0]
    )
    far, partner_below = add_half(far, to_far, 0), add_half(partner_below, to_below, 1)
    to_above, to_partner, to_above_too = up(far), down(partner_below), cross(partner_above)
    near_parts = sums(
        "near_rest",
        constants,
        near,
        rest,
        near_held,
        rows_out=rows,
        after=[far, partner_below],
    )
    own, partner, above, below = [near_parts[at : at + 2] for at in range(0, len(near_parts), 2)]
    partner = add_halves(partner, to_partner)
    above = add_halves(above, to_above, to_above_too)
    carried = [own[0], down(below[0]), cross(partner[0]), up(above[0])]
    handed = [to_core(own[1]), down_over(below[1]), cross_over(partner[1]), up_over(above[1])]
    image_grad, text_grad = through_norms(core, picture_vectors, caption_vectors, carried, handed)
    return image_grad, text_grad


def solution(mesh):
    return jax.shard_map(
        on_device,
        mesh=mesh,
        in_specs=(P(("blk", "grp"), None), P(("blk", "grp"), None), P(), P(), P()),
        out_specs=(P(("blk", "grp"), None), P(("blk", "grp"), None)),
        check_vma=False,
    )
```

```python
from functools import partial

import jax
import jax.numpy as jnp
from jax import lax
from jax.experimental import pallas as pl
from jax.experimental.pallas import tpu as pltpu
from jax.sharding import PartitionSpec as P

RING = 4
CORES = 2
TILE = 256
VMEM_BYTES = 24 * 1024 * 1024


def place(x, y, z, core):
    blk = ((x % 2) * RING + y) * CORES + core
    return blk * 8 + z * 2 + x // 2


def sender(move):
    pairs = [
        (place(x, y, z, core), place(*move(x, y, z, core)))
        for x in range(RING)
        for y in range(RING)
        for z in range(RING)
        for core in range(CORES)
    ]
    return lambda value: lax.ppermute(value, ("blk", "grp"), pairs)


def ring(steps):
    return sender(
        lambda x, y, z, c: (x, y, (z + steps) % RING, c) if c else (x, (y + steps) % RING, z, c)
    )


to_core = sender(lambda x, y, z, c: (x, y, z, 1 - c))
cross = sender(lambda x, y, z, c: (3 - x if c else x ^ 1, y, z, c))
up, down = ring(1), ring(RING - 1)


def call(name, body, out_shape, operands, flops, scalars=(), after=(), scratch=()):
    moved = sum(2 * value.size for value in operands) + sum(2 * shape.size for shape in out_shape)
    out = pl.pallas_call(
        lambda *refs: body(*refs[len(after) :]),
        name=name,
        out_shape=out_shape,
        in_specs=[pl.BlockSpec(memory_space=pl.ANY)] * len(after)
        + [pl.BlockSpec(memory_space=pltpu.SMEM)] * len(scalars)
        + [pl.BlockSpec(memory_space=pltpu.VMEM)] * len(operands),
        scratch_shapes=list(scratch),
        compiler_params=pltpu.CompilerParams(vmem_limit_bytes=VMEM_BYTES),
        cost_estimate=pl.CostEstimate(flops=flops // 64, bytes_accessed=moved // 64, transcendentals=0),
    )(*after, *scalars, *operands)
    return list(out)


def array(rows, columns):
    return jax.ShapeDtypeStruct((rows, columns), jnp.bfloat16)


def total_of(terms):
    total = terms[0].astype(jnp.float32)
    for term in terms[1:]:
        total = total + term.astype(jnp.float32)
    return total


def add(*terms, flops=0, after=()):
    def body(*refs):
        refs[-1][...] = total_of([ref[...] for ref in refs[:-1]]).astype(jnp.bfloat16)

    return call("add", body, [array(*terms[0].shape)], terms, flops, after=after)[0]


def unit_of(values):
    inverse = lax.rsqrt(jnp.sum(values * values, axis=1, keepdims=True) + 1e-06)
    return values * inverse, inverse


def unit_halves(core, parameters, batch_total, picture, caption):
    def body(core, warmth, score_offset, multiplier, picture, caption, keep, give, constants):
        scale = jnp.exp(jnp.full((1, TILE), warmth[0], jnp.float32))
        constants[0:1, :] = 0.5 * scale
        constants[1:2, :] = jnp.full((1, TILE), 0.5 * score_offset[0], jnp.float32)
        constants[2:3, :] = 0.5 * (multiplier[0] / batch_total * scale)

        def fill(carried, handed):
            keep[...] = unit_of(carried[...].astype(jnp.float32))[0].astype(jnp.bfloat16)
            give[...] = unit_of(handed[...].astype(jnp.float32))[0].astype(jnp.bfloat16)

        @pl.when(core[0] == 0)
        def _():
            fill(caption, picture)

        @pl.when(core[0] != 0)
        def _():
            fill(picture, caption)

    shapes = [array(*picture.shape)] * 2 + [jax.ShapeDtypeStruct((8, TILE), jnp.float32)]
    return call("units", body, shapes, [picture, caption], 6 * picture.size, [core, *parameters])


def pack(*blocks):
    rows, feature = blocks[0].shape

    def body(*refs):
        for at, ref in enumerate(refs[:-1]):
            refs[-1][pl.ds(at * rows, rows), :] = ref[...]

    return call("pack", body, [array(len(blocks) * rows, feature)], blocks, rows * feature)[0]


def stacked(refs):
    return jnp.concatenate([ref[...] for ref in refs], axis=0)


def sums(name, constants, left, right, held=None, own=False, rows_out=None, after=()):
    feature = left[0].shape[1]
    count, others = sum(ref.shape[0] for ref in left), sum(ref.shape[0] for ref in right)
    blocks = 1 if rows_out is None else count // rows_out

    def body(constants, *refs):
        left_refs, right_refs = refs[: len(left)], refs[len(left) :][: len(right)]
        refs = refs[len(left) + len(right) :]
        out, grads = refs[-1 - blocks : -1], refs[-1]
        slope, shift, factor = constants[0:1, :], constants[1:2, :], constants[2:3, :]
        tiles = [
            (ref, first)
            for ref, block in zip(right_refs, right)
            for first in range(0, block.shape[0], TILE)
        ]

        def scores(tile):
            ref, first = tile
            return lax.dot_general(
                stacked(left_refs),
                ref[pl.ds(first, TILE), :],
                (((1,), (1,)), ((), ())),
                preferred_element_type=jnp.float32,
            )

        upcoming = scores(tiles[0])
        for index in range(len(tiles)):
            current = upcoming
            if index + 1 < len(tiles):
                upcoming = scores(tiles[index + 1])
            bent = jnp.tanh(current * slope + shift) * factor
            offset = factor
            if own and index == 0:
                row = lax.broadcasted_iota(jnp.int32, bent.shape, 0)
                column = lax.broadcasted_iota(jnp.int32, bent.shape, 1)
                half = TILE // 2
                partner = jnp.where(row < half, row + half, row - half)
                paired = jnp.logical_and(column == partner, row < TILE)
                offset = jnp.where(paired, -factor, factor)
            grads[:, pl.ds(index * TILE, TILE)] = (bent + offset).astype(jnp.bfloat16)
        total = jnp.dot(grads[...], stacked(right_refs), preferred_element_type=jnp.float32)
        if held is not None:
            total = total + refs[0][...]
        if rows_out is None:
            out[0][...] = total
        else:
            for at, ref in enumerate(out):
                ref[...] = total[at * rows_out : (at + 1) * rows_out].astype(jnp.bfloat16)

    shapes = (
        [jax.ShapeDtypeStruct((count, feature), jnp.float32)]
        if rows_out is None
        else [array(rows_out, feature)] * blocks
    )
    return call(
        name,
        body,
        shapes,
        [constants, *left, *right] + ([] if held is None else [held]),
        4 * count * others * feature,
        (),
        after,
        [pltpu.VMEM((count, others), jnp.bfloat16)],
    )


def add_half(whole, part, half, flops=0, after=()):
    rows = part.shape[0]

    def body(whole, part, out):
        out[pl.ds((1 - half) * rows, rows), :] = whole[pl.ds((1 - half) * rows, rows), :]
        here = pl.ds(half * rows, rows)
        out[here, :] = total_of([whole[here, :], part[...]]).astype(jnp.bfloat16)

    return call("add_half", body, [array(*whole.shape)], [whole, part], flops, after=after)[0]


def through_norms(core, picture, caption, terms):
    rows, feature = picture.shape

    def give_body(*refs):
        total = total_of([ref[pl.ds(rows, rows), :] for ref in refs[:-1]])
        refs[-1][...] = total.astype(jnp.bfloat16)

    got = to_core(call("give", give_body, [array(rows, feature)], terms, 4 * rows * feature)[0])

    def body(core, picture, caption, got, *refs):
        kept, (image_out, text_out) = refs[:-2], refs[-2:]

        def finish(raw, direct, out):
            unit, inverse = unit_of(raw[...].astype(jnp.float32))
            along = jnp.sum(unit * direct, axis=1, keepdims=True)
            out[...] = (inverse * (direct - unit * along)).astype(jnp.bfloat16)

        def direct_kept():
            return total_of([ref[pl.ds(0, rows), :] for ref in kept])

        @pl.when(core[0] == 0)
        def _():
            finish(picture, got[...].astype(jnp.float32), image_out)
            finish(caption, direct_kept(), text_out)

        @pl.when(core[0] != 0)
        def _():
            finish(picture, direct_kept(), image_out)
            finish(caption, got[...].astype(jnp.float32), text_out)

    return call(
        "final",
        body,
        [array(rows, feature)] * 2,
        [picture, caption, got, *terms],
        20 * rows * feature,
        [core],
    )


def on_device(
    picture_vectors, caption_vectors, ln_inverse_warmth, score_offset, objective_multiplier
):
    batch_total = picture_vectors.shape[0] * lax.axis_size(("blk", "grp"))
    parameters = [
        value.reshape(1) for value in (ln_inverse_warmth, score_offset, objective_multiplier)
    ]
    core = (lax.axis_index("blk") & (CORES - 1)).reshape(1)
    rows = picture_vectors.shape[0]
    keep, give, constants = unit_halves(
        core, parameters, batch_total, picture_vectors, caption_vectors
    )
    own = jnp.concatenate([keep, to_core(give)], axis=0)
    partner, below, above = cross(own), up(own), down(own)
    partner_above, partner_below, far = cross(above), up(partner), down(above)
    near = [own, partner, above, below]
    near_other = [to_core(block) for block in near]
    near_held = sums("near", constants, near, near_other, own=True)[0]
    partner_below, near_held = lax.optimization_barrier((partner_below, near_held))
    far, near_held = lax.optimization_barrier((far, near_held))
    last = cross(far[:rows]), up(partner_below[rows:])
    middle = [partner_above, partner_below, far]
    middle_other = [to_core(block) for block in middle]
    middle_held = sums("middle", constants, middle, near_other)[0]
    *last, middle_held = lax.optimization_barrier((*last, middle_held))
    last = pack(*last)
    last_other = to_core(last)
    last_held = sums("last", constants, [last], [*near_other, *middle_other])[0]

    last_0, last_1 = sums("last_rest", constants, [last], [last_other], last_held, rows_out=rows)
    to_far, to_below = cross(last_0), down(last_1)
    rest = [*middle_other, last_other]
    partner_above, partner_below, far = sums(
        "middle_rest", constants, middle, rest, middle_held, rows_out=2 * rows, after=[last_0]
    )
    far, partner_below = add_half(far, to_far, 0), add_half(partner_below, to_below, 1)
    to_above, to_partner, to_above_too = up(far), down(partner_below), cross(partner_above)
    own, partner, above, below = sums(
        "near_rest",
        constants,
        near,
        rest,
        near_held,
        rows_out=2 * rows,
        after=[far, partner_below],
    )
    above, partner = add(above, to_above, to_above_too), add(partner, to_partner)
    terms = [own, up(above), down(below), cross(partner)]
    image_grad, text_grad = through_norms(core, picture_vectors, caption_vectors, terms)
    return image_grad, text_grad


def solution(mesh):
    return jax.shard_map(
        on_device,
        mesh=mesh,
        in_specs=(P(("blk", "grp"), None), P(("blk", "grp"), None), P(), P(), P()),
        out_specs=(P(("blk", "grp"), None), P(("blk", "grp"), None)),
        check_vma=False,
    )
```

```python
from functools import partial

import jax
import jax.numpy as jnp
from jax import lax
from jax.experimental import pallas as pl
from jax.experimental.pallas import tpu as pltpu
from jax.sharding import PartitionSpec as P

RING = 4
CORES = 2
TILE = 256
SEND_FLOPS = 10**12
VMEM_BYTES = 24 * 1024 * 1024


def place(x, y, z, core):
    blk = ((x % 2) * RING + y) * CORES + core
    return blk * 8 + z * 2 + x // 2


def sender(move):
    pairs = [
        (place(x, y, z, core), place(*move(x, y, z, core)))
        for x in range(RING)
        for y in range(RING)
        for z in range(RING)
        for core in range(CORES)
    ]
    return lambda value: lax.ppermute(value, ("blk", "grp"), pairs)


def ring(steps):
    return sender(
        lambda x, y, z, c: (x, y, (z + steps) % RING, c) if c else (x, (y + steps) % RING, z, c)
    )


to_core = sender(lambda x, y, z, c: (x, y, z, 1 - c))
cross = sender(lambda x, y, z, c: (3 - x if c else x ^ 1, y, z, c))
up, down = ring(1), ring(RING - 1)


def call(name, body, out_shape, operands, flops, scalars=(), after=(), scratch=()):
    moved = sum(2 * value.size for value in operands) + sum(2 * shape.size for shape in out_shape)
    out = pl.pallas_call(
        lambda *refs: body(*refs[len(after) :]),
        name=name,
        out_shape=out_shape,
        in_specs=[pl.BlockSpec(memory_space=pl.ANY)] * len(after)
        + [pl.BlockSpec(memory_space=pltpu.SMEM)] * len(scalars)
        + [pl.BlockSpec(memory_space=pltpu.VMEM)] * len(operands),
        scratch_shapes=list(scratch),
        compiler_params=pltpu.CompilerParams(vmem_limit_bytes=VMEM_BYTES),
        cost_estimate=pl.CostEstimate(flops=flops // 64, bytes_accessed=moved // 64, transcendentals=0),
    )(*after, *scalars, *operands)
    return list(out)


def array(rows, columns):
    return jax.ShapeDtypeStruct((rows, columns), jnp.bfloat16)


def total_of(terms):
    total = terms[0].astype(jnp.float32)
    for term in terms[1:]:
        total = total + term.astype(jnp.float32)
    return total


def add(*terms, flops=0, after=()):
    def body(*refs):
        refs[-1][...] = total_of([ref[...] for ref in refs[:-1]]).astype(jnp.bfloat16)

    return call("add", body, [array(*terms[0].shape)], terms, flops, after=after)[0]


def unit_of(values):
    inverse = lax.rsqrt(jnp.sum(values * values, axis=1, keepdims=True) + 1e-06)
    return values * inverse, inverse


def unit_halves(core, parameters, batch_total, picture, caption):
    def body(core, warmth, score_offset, multiplier, picture, caption, keep, give, constants):
        scale = jnp.exp(jnp.full((1, TILE), warmth[0], jnp.float32))
        constants[0:1, :] = 0.5 * scale
        constants[1:2, :] = jnp.full((1, TILE), 0.5 * score_offset[0], jnp.float32)
        constants[2:3, :] = 0.5 * (multiplier[0] / batch_total * scale)

        def fill(carried, handed):
            keep[...] = unit_of(carried[...].astype(jnp.float32))[0].astype(jnp.bfloat16)
            give[...] = unit_of(handed[...].astype(jnp.float32))[0].astype(jnp.bfloat16)

        @pl.when(core[0] == 0)
        def _():
            fill(caption, picture)

        @pl.when(core[0] != 0)
        def _():
            fill(picture, caption)

    shapes = [array(*picture.shape)] * 2 + [jax.ShapeDtypeStruct((8, TILE), jnp.float32)]
    return call("units", body, shapes, [picture, caption], 6 * picture.size, [core, *parameters])


def pack(*blocks):
    rows, feature = blocks[0].shape

    def body(*refs):
        for at, ref in enumerate(refs[:-1]):
            refs[-1][pl.ds(at * rows, rows), :] = ref[...]

    return call("pack", body, [array(len(blocks) * rows, feature)], blocks, rows * feature)[0]


def stacked(refs):
    return jnp.concatenate([ref[...] for ref in refs], axis=0)


def sums(name, constants, left, right, held=None, own=False, rows_out=None, after=()):
    feature = left[0].shape[1]
    count, others = sum(ref.shape[0] for ref in left), sum(ref.shape[0] for ref in right)
    blocks = 1 if rows_out is None else count // rows_out

    def body(constants, *refs):
        left_refs, right_refs = refs[: len(left)], refs[len(left) :][: len(right)]
        refs = refs[len(left) + len(right) :]
        out, grads = refs[-1 - blocks : -1], refs[-1]
        slope, shift, factor = constants[0:1, :], constants[1:2, :], constants[2:3, :]
        tiles = [
            (ref, first)
            for ref, block in zip(right_refs, right)
            for first in range(0, block.shape[0], TILE)
        ]

        def scores(tile):
            ref, first = tile
            return lax.dot_general(
                stacked(left_refs),
                ref[pl.ds(first, TILE), :],
                (((1,), (1,)), ((), ())),
                preferred_element_type=jnp.float32,
            )

        upcoming = scores(tiles[0])
        for index in range(len(tiles)):
            current = upcoming
            if index + 1 < len(tiles):
                upcoming = scores(tiles[index + 1])
            bent = jnp.tanh(current * slope + shift) * factor
            offset = factor
            if own and index == 0:
                row = lax.broadcasted_iota(jnp.int32, bent.shape, 0)
                column = lax.broadcasted_iota(jnp.int32, bent.shape, 1)
                half = TILE // 2
                partner = jnp.where(row < half, row + half, row - half)
                paired = jnp.logical_and(column == partner, row < TILE)
                offset = jnp.where(paired, -factor, factor)
            grads[:, pl.ds(index * TILE, TILE)] = (bent + offset).astype(jnp.bfloat16)
        total = jnp.dot(grads[...], stacked(right_refs), preferred_element_type=jnp.float32)
        if held is not None:
            total = total + refs[0][...]
        if rows_out is None:
            out[0][...] = total
        else:
            for at, ref in enumerate(out):
                ref[...] = total[at * rows_out : (at + 1) * rows_out].astype(jnp.bfloat16)

    shapes = (
        [jax.ShapeDtypeStruct((count, feature), jnp.float32)]
        if rows_out is None
        else [array(rows_out, feature)] * blocks
    )
    return call(
        name,
        body,
        shapes,
        [constants, *left, *right] + ([] if held is None else [held]),
        4 * count * others * feature,
        (),
        after,
        [pltpu.VMEM((count, others), jnp.bfloat16)],
    )


def add_half(whole, part, half, flops=0, after=()):
    rows = part.shape[0]

    def body(whole, part, out):
        out[pl.ds((1 - half) * rows, rows), :] = whole[pl.ds((1 - half) * rows, rows), :]
        here = pl.ds(half * rows, rows)
        out[here, :] = total_of([whole[here, :], part[...]]).astype(jnp.bfloat16)

    return call("add_half", body, [array(*whole.shape)], [whole, part], flops, after=after)[0]


def through_norms(core, picture, caption, terms):
    rows, feature = picture.shape

    def give_body(*refs):
        total = total_of([ref[pl.ds(rows, rows), :] for ref in refs[:-1]])
        refs[-1][...] = total.astype(jnp.bfloat16)

    got = to_core(call("give", give_body, [array(rows, feature)], terms, 4 * rows * feature)[0])

    def body(core, picture, caption, got, *refs):
        kept, (image_out, text_out) = refs[:-2], refs[-2:]

        def finish(raw, direct, out):
            unit, inverse = unit_of(raw[...].astype(jnp.float32))
            along = jnp.sum(unit * direct, axis=1, keepdims=True)
            out[...] = (inverse * (direct - unit * along)).astype(jnp.bfloat16)

        def direct_kept():
            return total_of([ref[pl.ds(0, rows), :] for ref in kept])

        @pl.when(core[0] == 0)
        def _():
            finish(picture, got[...].astype(jnp.float32), image_out)
            finish(caption, direct_kept(), text_out)

        @pl.when(core[0] != 0)
        def _():
            finish(picture, direct_kept(), image_out)
            finish(caption, got[...].astype(jnp.float32), text_out)

    return call(
        "final",
        body,
        [array(rows, feature)] * 2,
        [picture, caption, got, *terms],
        20 * rows * feature,
        [core],
    )


def on_device(
    picture_vectors, caption_vectors, ln_inverse_warmth, score_offset, objective_multiplier
):
    batch_total = picture_vectors.shape[0] * lax.axis_size(("blk", "grp"))
    parameters = [
        value.reshape(1) for value in (ln_inverse_warmth, score_offset, objective_multiplier)
    ]
    core = (lax.axis_index("blk") & (CORES - 1)).reshape(1)
    rows = picture_vectors.shape[0]
    keep, give, constants = unit_halves(
        core, parameters, batch_total, picture_vectors, caption_vectors
    )
    own = jnp.concatenate([keep, to_core(give)], axis=0)
    partner, below, above = cross(own), up(own), down(own)
    partner_above, partner_below, far = cross(above), up(partner), down(above)
    near = [own, partner, above, below]
    near_other = [to_core(block) for block in near]
    near_held = sums("near", constants, near, near_other, own=True)[0]
    partner_below, near_held = lax.optimization_barrier((partner_below, near_held))
    far, near_held = lax.optimization_barrier((far, near_held))
    last = cross(far[:rows]), up(partner_below[rows:])
    middle = [partner_above, partner_below, far]
    middle_other = [to_core(block) for block in middle]
    middle_held = sums("middle", constants, middle, near_other)[0]
    *last, middle_held = lax.optimization_barrier((*last, middle_held))
    last = pack(*last)
    last_other = to_core(last)
    last_held = sums("last", constants, [last], [*near_other, *middle_other])[0]

    last_0, last_1 = sums("last_rest", constants, [last], [last_other], last_held, rows_out=rows)
    to_far, to_below = cross(last_0), down(last_1)
    rest = [*middle_other, last_other]
    partner_above, partner_below, far = sums(
        "middle_rest", constants, middle, rest, middle_held, rows_out=2 * rows, after=[last_0]
    )
    far = add_half(far, to_far, 0, flops=SEND_FLOPS)
    partner_below = add_half(partner_below, to_below, 1, flops=SEND_FLOPS)
    to_above, to_partner, to_above_too = up(far), down(partner_below), cross(partner_above)
    own, partner, above, below = sums(
        "near_rest",
        constants,
        near,
        rest,
        near_held,
        rows_out=2 * rows,
        after=[far, partner_below],
    )
    above = add(add(above, to_above_too, flops=SEND_FLOPS), to_above)
    partner = add(partner, to_partner)
    terms = [own, up(above), down(below), cross(partner)]
    image_grad, text_grad = through_norms(core, picture_vectors, caption_vectors, terms)
    return image_grad, text_grad


def solution(mesh):
    return jax.shard_map(
        on_device,
        mesh=mesh,
        in_specs=(P(("blk", "grp"), None), P(("blk", "grp"), None), P(), P(), P()),
        out_specs=(P(("blk", "grp"), None), P(("blk", "grp"), None)),
        check_vma=False,
    )
```

```python
from functools import partial

import jax
import jax.numpy as jnp
from jax import lax
from jax.experimental import pallas as pl
from jax.experimental.pallas import tpu as pltpu
from jax.sharding import PartitionSpec as P

RING = 4
CORES = 2
TILE = 256
SEND_FLOPS = 10**12
VMEM_BYTES = 24 * 1024 * 1024


def place(x, y, z, core):
    blk = ((x % 2) * RING + y) * CORES + core
    return blk * 8 + z * 2 + x // 2


def sender(move):
    pairs = [
        (place(x, y, z, core), place(*move(x, y, z, core)))
        for x in range(RING)
        for y in range(RING)
        for z in range(RING)
        for core in range(CORES)
    ]
    return lambda value: lax.ppermute(value, ("blk", "grp"), pairs)


def ring(steps):
    return sender(
        lambda x, y, z, c: (x, y, (z + steps) % RING, c) if c else (x, (y + steps) % RING, z, c)
    )


to_core = sender(lambda x, y, z, c: (x, y, z, 1 - c))
cross = sender(lambda x, y, z, c: (3 - x if c else x ^ 1, y, z, c))
up, down = ring(1), ring(RING - 1)


def call(name, body, out_shape, operands, flops, scalars=(), after=(), scratch=()):
    moved = sum(2 * value.size for value in operands) + sum(2 * shape.size for shape in out_shape)
    out = pl.pallas_call(
        lambda *refs: body(*refs[len(after) :]),
        name=name,
        out_shape=out_shape,
        in_specs=[pl.BlockSpec(memory_space=pl.ANY)] * len(after)
        + [pl.BlockSpec(memory_space=pltpu.SMEM)] * len(scalars)
        + [pl.BlockSpec(memory_space=pltpu.VMEM)] * len(operands),
        scratch_shapes=list(scratch),
        compiler_params=pltpu.CompilerParams(vmem_limit_bytes=VMEM_BYTES),
        cost_estimate=pl.CostEstimate(flops=flops // 64, bytes_accessed=moved // 64, transcendentals=0),
    )(*after, *scalars, *operands)
    return list(out)


def array(rows, columns):
    return jax.ShapeDtypeStruct((rows, columns), jnp.bfloat16)


def total_of(terms):
    total = terms[0].astype(jnp.float32)
    for term in terms[1:]:
        total = total + term.astype(jnp.float32)
    return total


def add(*terms, flops=0, after=()):
    def body(*refs):
        refs[-1][...] = total_of([ref[...] for ref in refs[:-1]]).astype(jnp.bfloat16)

    return call("add", body, [array(*terms[0].shape)], terms, flops, after=after)[0]


def unit_of(values):
    inverse = lax.rsqrt(jnp.sum(values * values, axis=1, keepdims=True) + 1e-06)
    return values * inverse, inverse


def unit_halves(core, parameters, batch_total, picture, caption):
    def body(core, warmth, score_offset, multiplier, picture, caption, keep, give, constants):
        scale = jnp.exp(jnp.full((1, TILE), warmth[0], jnp.float32))
        constants[0:1, :] = 0.5 * scale
        constants[1:2, :] = jnp.full((1, TILE), 0.5 * score_offset[0], jnp.float32)
        constants[2:3, :] = 0.5 * (multiplier[0] / batch_total * scale)

        def fill(carried, handed):
            keep[...] = unit_of(carried[...].astype(jnp.float32))[0].astype(jnp.bfloat16)
            give[...] = unit_of(handed[...].astype(jnp.float32))[0].astype(jnp.bfloat16)

        @pl.when(core[0] == 0)
        def _():
            fill(caption, picture)

        @pl.when(core[0] != 0)
        def _():
            fill(picture, caption)

    shapes = [array(*picture.shape)] * 2 + [jax.ShapeDtypeStruct((8, TILE), jnp.float32)]
    return call("units", body, shapes, [picture, caption], 6 * picture.size, [core, *parameters])


def pack(*blocks):
    rows, feature = blocks[0].shape

    def body(*refs):
        for at, ref in enumerate(refs[:-1]):
            refs[-1][pl.ds(at * rows, rows), :] = ref[...]

    return call("pack", body, [array(len(blocks) * rows, feature)], blocks, rows * feature)[0]


def stacked(refs):
    return jnp.concatenate([ref[...] for ref in refs], axis=0)


def sums(name, constants, left, right, held=None, own=False, rows_out=None, after=()):
    feature = left[0].shape[1]
    count, others = sum(ref.shape[0] for ref in left), sum(ref.shape[0] for ref in right)
    blocks = 1 if rows_out is None else count // rows_out

    def body(constants, *refs):
        left_refs, right_refs = refs[: len(left)], refs[len(left) :][: len(right)]
        refs = refs[len(left) + len(right) :]
        out, grads = refs[-1 - blocks : -1], refs[-1]
        slope, shift, factor = constants[0:1, :], constants[1:2, :], constants[2:3, :]
        tiles = [
            (ref, first)
            for ref, block in zip(right_refs, right)
            for first in range(0, block.shape[0], TILE)
        ]

        def scores(tile):
            ref, first = tile
            return lax.dot_general(
                stacked(left_refs),
                ref[pl.ds(first, TILE), :],
                (((1,), (1,)), ((), ())),
                preferred_element_type=jnp.float32,
            )

        upcoming = scores(tiles[0])
        for index in range(len(tiles)):
            current = upcoming
            if index + 1 < len(tiles):
                upcoming = scores(tiles[index + 1])
            bent = jnp.tanh(current * slope + shift) * factor
            offset = factor
            if own and index == 0:
                row = lax.broadcasted_iota(jnp.int32, bent.shape, 0)
                column = lax.broadcasted_iota(jnp.int32, bent.shape, 1)
                half = TILE // 2
                partner = jnp.where(row < half, row + half, row - half)
                paired = jnp.logical_and(column == partner, row < TILE)
                offset = jnp.where(paired, -factor, factor)
            grads[:, pl.ds(index * TILE, TILE)] = (bent + offset).astype(jnp.bfloat16)
        total = jnp.dot(grads[...], stacked(right_refs), preferred_element_type=jnp.float32)
        if held is not None:
            total = total + refs[0][...]
        if rows_out is None:
            out[0][...] = total
        else:
            for at, ref in enumerate(out):
                ref[...] = total[at * rows_out : (at + 1) * rows_out].astype(jnp.bfloat16)

    shapes = (
        [jax.ShapeDtypeStruct((count, feature), jnp.float32)]
        if rows_out is None
        else [array(rows_out, feature)] * blocks
    )
    return call(
        name,
        body,
        shapes,
        [constants, *left, *right] + ([] if held is None else [held]),
        4 * count * others * feature,
        (),
        after,
        [pltpu.VMEM((count, others), jnp.bfloat16)],
    )


def add_half(whole, part, half, flops=0, after=()):
    rows = part.shape[0]

    def body(whole, part, out):
        out[pl.ds((1 - half) * rows, rows), :] = whole[pl.ds((1 - half) * rows, rows), :]
        here = pl.ds(half * rows, rows)
        out[here, :] = total_of([whole[here, :], part[...]]).astype(jnp.bfloat16)

    return call("add_half", body, [array(*whole.shape)], [whole, part], flops, after=after)[0]


def through_norms(core, picture, caption, terms):
    rows, feature = picture.shape

    def give_body(*refs):
        total = total_of([ref[pl.ds(rows, rows), :] for ref in refs[:-1]])
        refs[-1][...] = total.astype(jnp.bfloat16)

    got = to_core(call("give", give_body, [array(rows, feature)], terms, 4 * rows * feature)[0])

    def body(core, picture, caption, got, *refs):
        kept, (image_out, text_out) = refs[:-2], refs[-2:]

        def finish(raw, direct, out):
            unit, inverse = unit_of(raw[...].astype(jnp.float32))
            along = jnp.sum(unit * direct, axis=1, keepdims=True)
            out[...] = (inverse * (direct - unit * along)).astype(jnp.bfloat16)

        def direct_kept():
            return total_of([ref[pl.ds(0, rows), :] for ref in kept])

        @pl.when(core[0] == 0)
        def _():
            finish(picture, got[...].astype(jnp.float32), image_out)
            finish(caption, direct_kept(), text_out)

        @pl.when(core[0] != 0)
        def _():
            finish(picture, direct_kept(), image_out)
            finish(caption, got[...].astype(jnp.float32), text_out)

    return call(
        "final",
        body,
        [array(rows, feature)] * 2,
        [picture, caption, got, *terms],
        20 * rows * feature,
        [core],
    )


def on_device(
    picture_vectors, caption_vectors, ln_inverse_warmth, score_offset, objective_multiplier
):
    batch_total = picture_vectors.shape[0] * lax.axis_size(("blk", "grp"))
    parameters = [
        value.reshape(1) for value in (ln_inverse_warmth, score_offset, objective_multiplier)
    ]
    core = (lax.axis_index("blk") & (CORES - 1)).reshape(1)
    rows = picture_vectors.shape[0]
    keep, give, constants = unit_halves(
        core, parameters, batch_total, picture_vectors, caption_vectors
    )
    own = jnp.concatenate([keep, to_core(give)], axis=0)
    partner, below, above = cross(own), up(own), down(own)
    partner_above, partner_below, far = cross(above), up(partner), down(above)
    near = [own, partner, above, below]
    near_other = [to_core(block) for block in near]
    near_held = sums("near", constants, near, near_other, own=True)[0]
    partner_below, near_held = lax.optimization_barrier((partner_below, near_held))
    far, near_held = lax.optimization_barrier((far, near_held))
    last = cross(far[:rows]), up(partner_below[rows:])
    middle = [partner_above, partner_below, far]
    middle_other = [to_core(block) for block in middle]
    middle_held = sums("middle", constants, middle, near_other)[0]
    *last, middle_held = lax.optimization_barrier((*last, middle_held))
    last = pack(*last)
    last_other = to_core(last)
    last_held = sums("last", constants, [last], [*near_other, *middle_other])[0]

    last_0, last_1 = sums("last_rest", constants, [last], [last_other], last_held, rows_out=rows)
    to_far, to_below = cross(last_0), down(last_1)
    rest = [*middle_other, last_other]
    partner_above, partner_below, far = sums(
        "middle_rest", constants, middle, rest, middle_held, rows_out=2 * rows, after=[last_0]
    )
    partner_below = add_half(partner_below, to_below, 1, flops=SEND_FLOPS)
    far = add_half(far, to_far, 0, flops=SEND_FLOPS, after=[partner_below])
    to_above, to_partner, to_above_too = up(far), down(partner_below), cross(partner_above)
    own, partner, above, below = sums(
        "near_rest",
        constants,
        near,
        rest,
        near_held,
        rows_out=2 * rows,
        after=[far, partner_below],
    )
    above = add(add(above, to_above_too, flops=SEND_FLOPS), to_above)
    partner = add(partner, to_partner)
    terms = [own, up(above), down(below), cross(partner)]
    image_grad, text_grad = through_norms(core, picture_vectors, caption_vectors, terms)
    return image_grad, text_grad


def solution(mesh):
    return jax.shard_map(
        on_device,
        mesh=mesh,
        in_specs=(P(("blk", "grp"), None), P(("blk", "grp"), None), P(), P(), P()),
        out_specs=(P(("blk", "grp"), None), P(("blk", "grp"), None)),
        check_vma=False,
    )
```

```python
from functools import partial

import jax
import jax.numpy as jnp
from jax import lax
from jax.experimental import pallas as pl
from jax.experimental.pallas import tpu as pltpu
from jax.sharding import PartitionSpec as P

RING = 4
CORES = 2
TILE = 256
SEND_FLOPS = 10**12
VMEM_BYTES = 24 * 1024 * 1024


def place(x, y, z, core):
    blk = ((x % 2) * RING + y) * CORES + core
    return blk * 8 + z * 2 + x // 2


def sender(move):
    pairs = [
        (place(x, y, z, core), place(*move(x, y, z, core)))
        for x in range(RING)
        for y in range(RING)
        for z in range(RING)
        for core in range(CORES)
    ]
    return lambda value: lax.ppermute(value, ("blk", "grp"), pairs)


def ring(steps):
    return sender(
        lambda x, y, z, c: (x, y, (z + steps) % RING, c) if c else (x, (y + steps) % RING, z, c)
    )


to_core = sender(lambda x, y, z, c: (x, y, z, 1 - c))
cross = sender(lambda x, y, z, c: (3 - x if c else x ^ 1, y, z, c))
up, down = ring(1), ring(RING - 1)


def call(name, body, out_shape, operands, flops, scalars=(), after=(), scratch=()):
    moved = sum(2 * value.size for value in operands) + sum(2 * shape.size for shape in out_shape)
    out = pl.pallas_call(
        lambda *refs: body(*refs[len(after) :]),
        name=name,
        out_shape=out_shape,
        in_specs=[pl.BlockSpec(memory_space=pl.ANY)] * len(after)
        + [pl.BlockSpec(memory_space=pltpu.SMEM)] * len(scalars)
        + [pl.BlockSpec(memory_space=pltpu.VMEM)] * len(operands),
        scratch_shapes=list(scratch),
        compiler_params=pltpu.CompilerParams(vmem_limit_bytes=VMEM_BYTES),
        cost_estimate=pl.CostEstimate(flops=flops // 64, bytes_accessed=moved // 64, transcendentals=0),
    )(*after, *scalars, *operands)
    return list(out)


def array(rows, columns):
    return jax.ShapeDtypeStruct((rows, columns), jnp.bfloat16)


def total_of(terms):
    total = terms[0].astype(jnp.float32)
    for term in terms[1:]:
        total = total + term.astype(jnp.float32)
    return total


def add(*terms, flops=0, after=()):
    def body(*refs):
        refs[-1][...] = total_of([ref[...] for ref in refs[:-1]]).astype(jnp.bfloat16)

    return call("add", body, [array(*terms[0].shape)], terms, flops, after=after)[0]


def unit_of(values):
    inverse = lax.rsqrt(jnp.sum(values * values, axis=1, keepdims=True) + 1e-06)
    return values * inverse, inverse


def unit_halves(core, parameters, batch_total, picture, caption):
    def body(core, warmth, score_offset, multiplier, picture, caption, keep, give, constants):
        scale = jnp.exp(jnp.full((1, TILE), warmth[0], jnp.float32))
        constants[0:1, :] = 0.5 * scale
        constants[1:2, :] = jnp.full((1, TILE), 0.5 * score_offset[0], jnp.float32)
        constants[2:3, :] = 0.5 * (multiplier[0] / batch_total * scale)

        def fill(carried, handed):
            keep[...] = unit_of(carried[...].astype(jnp.float32))[0].astype(jnp.bfloat16)
            give[...] = unit_of(handed[...].astype(jnp.float32))[0].astype(jnp.bfloat16)

        @pl.when(core[0] == 0)
        def _():
            fill(caption, picture)

        @pl.when(core[0] != 0)
        def _():
            fill(picture, caption)

    shapes = [array(*picture.shape)] * 2 + [jax.ShapeDtypeStruct((8, TILE), jnp.float32)]
    return call("units", body, shapes, [picture, caption], 6 * picture.size, [core, *parameters])


def pack(*blocks):
    rows, feature = blocks[0].shape

    def body(*refs):
        for at, ref in enumerate(refs[:-1]):
            refs[-1][pl.ds(at * rows, rows), :] = ref[...]

    return call("pack", body, [array(len(blocks) * rows, feature)], blocks, rows * feature)[0]


def stacked(refs):
    return jnp.concatenate([ref[...] for ref in refs], axis=0)


def sums(name, constants, left, right, held=None, own=False, rows_out=None, after=()):
    feature = left[0].shape[1]
    count, others = sum(ref.shape[0] for ref in left), sum(ref.shape[0] for ref in right)
    blocks = 1 if rows_out is None else count // rows_out

    def body(constants, *refs):
        left_refs, right_refs = refs[: len(left)], refs[len(left) :][: len(right)]
        refs = refs[len(left) + len(right) :]
        out, grads = refs[-1 - blocks : -1], refs[-1]
        slope, shift, factor = constants[0:1, :], constants[1:2, :], constants[2:3, :]
        tiles = [
            (ref, first)
            for ref, block in zip(right_refs, right)
            for first in range(0, block.shape[0], TILE)
        ]

        def scores(tile):
            ref, first = tile
            return lax.dot_general(
                stacked(left_refs),
                ref[pl.ds(first, TILE), :],
                (((1,), (1,)), ((), ())),
                preferred_element_type=jnp.float32,
            )

        upcoming = scores(tiles[0])
        for index in range(len(tiles)):
            current = upcoming
            if index + 1 < len(tiles):
                upcoming = scores(tiles[index + 1])
            bent = jnp.tanh(current * slope + shift) * factor
            offset = factor
            if own and index == 0:
                row = lax.broadcasted_iota(jnp.int32, bent.shape, 0)
                column = lax.broadcasted_iota(jnp.int32, bent.shape, 1)
                half = TILE // 2
                partner = jnp.where(row < half, row + half, row - half)
                paired = jnp.logical_and(column == partner, row < TILE)
                offset = jnp.where(paired, -factor, factor)
            grads[:, pl.ds(index * TILE, TILE)] = (bent + offset).astype(jnp.bfloat16)
        total = jnp.dot(grads[...], stacked(right_refs), preferred_element_type=jnp.float32)
        if held is not None:
            total = total + refs[0][...]
        if rows_out is None:
            out[0][...] = total
        else:
            for at, ref in enumerate(out):
                ref[...] = total[at * rows_out : (at + 1) * rows_out].astype(jnp.bfloat16)

    shapes = (
        [jax.ShapeDtypeStruct((count, feature), jnp.float32)]
        if rows_out is None
        else [array(rows_out, feature)] * blocks
    )
    return call(
        name,
        body,
        shapes,
        [constants, *left, *right] + ([] if held is None else [held]),
        4 * count * others * feature,
        (),
        after,
        [pltpu.VMEM((count, others), jnp.bfloat16)],
    )


def add_half(whole, part, half, flops=0, after=()):
    rows = part.shape[0]

    def body(whole, part, out):
        out[pl.ds((1 - half) * rows, rows), :] = whole[pl.ds((1 - half) * rows, rows), :]
        here = pl.ds(half * rows, rows)
        out[here, :] = total_of([whole[here, :], part[...]]).astype(jnp.bfloat16)

    return call("add_half", body, [array(*whole.shape)], [whole, part], flops, after=after)[0]


def through_norms(core, picture, caption, terms):
    rows, feature = picture.shape

    def give_body(*refs):
        total = total_of([ref[pl.ds(rows, rows), :] for ref in refs[:-1]])
        refs[-1][...] = total.astype(jnp.bfloat16)

    got = to_core(call("give", give_body, [array(rows, feature)], terms, 4 * rows * feature)[0])

    def body(core, picture, caption, got, *refs):
        kept, (image_out, text_out) = refs[:-2], refs[-2:]

        def finish(raw, direct, out):
            unit, inverse = unit_of(raw[...].astype(jnp.float32))
            along = jnp.sum(unit * direct, axis=1, keepdims=True)
            out[...] = (inverse * (direct - unit * along)).astype(jnp.bfloat16)

        def direct_kept():
            return total_of([ref[pl.ds(0, rows), :] for ref in kept])

        @pl.when(core[0] == 0)
        def _():
            finish(picture, got[...].astype(jnp.float32), image_out)
            finish(caption, direct_kept(), text_out)

        @pl.when(core[0] != 0)
        def _():
            finish(picture, direct_kept(), image_out)
            finish(caption, got[...].astype(jnp.float32), text_out)

    return call(
        "final",
        body,
        [array(rows, feature)] * 2,
        [picture, caption, got, *terms],
        20 * rows * feature,
        [core],
    )


def on_device(
    picture_vectors, caption_vectors, ln_inverse_warmth, score_offset, objective_multiplier
):
    batch_total = picture_vectors.shape[0] * lax.axis_size(("blk", "grp"))
    parameters = [
        value.reshape(1) for value in (ln_inverse_warmth, score_offset, objective_multiplier)
    ]
    core = (lax.axis_index("blk") & (CORES - 1)).reshape(1)
    rows = picture_vectors.shape[0]
    keep, give, constants = unit_halves(
        core, parameters, batch_total, picture_vectors, caption_vectors
    )
    own = jnp.concatenate([keep, to_core(give)], axis=0)
    partner, below, above = cross(own), up(own), down(own)
    own_other, partner = lax.optimization_barrier((to_core(own), partner))
    partner_above, partner_below, far = cross(above), up(partner), down(above)
    lines = pack(above, below)
    near, near_other = [own, partner, lines], [own_other, to_core(partner), to_core(lines)]
    near_held = sums("near", constants, near, near_other, own=True)[0]
    partner_below, near_held = lax.optimization_barrier((partner_below, near_held))
    far, near_held = lax.optimization_barrier((far, near_held))
    last = cross(far[:rows]), up(partner_below[rows:])
    middle = [partner_above, partner_below, far]
    middle_other = [to_core(block) for block in middle]
    middle_held = sums("middle", constants, middle, near_other)[0]
    *last, middle_held = lax.optimization_barrier((*last, middle_held))
    last = pack(*last)
    last_other = to_core(last)
    last_held = sums("last", constants, [last], [*near_other, *middle_other])[0]

    last_0, last_1 = sums("last_rest", constants, [last], [last_other], last_held, rows_out=rows)
    to_far, to_below = cross(last_0), down(last_1)
    rest = [*middle_other, last_other]
    partner_above, partner_below, far = sums(
        "middle_rest", constants, middle, rest, middle_held, rows_out=2 * rows, after=[last_0]
    )
    partner_below = add_half(partner_below, to_below, 1, flops=SEND_FLOPS)
    far = add_half(far, to_far, 0, flops=SEND_FLOPS, after=[partner_below])
    to_above, to_partner, to_above_too = up(far), down(partner_below), cross(partner_above)
    own, partner, above, below = sums(
        "near_rest",
        constants,
        near,
        rest,
        near_held,
        rows_out=2 * rows,
        after=[far, partner_below],
    )
    above = add(add(above, to_above_too, flops=SEND_FLOPS), to_above)
    partner = add(partner, to_partner)
    terms = [own, up(above), down(below), cross(partner)]
    image_grad, text_grad = through_norms(core, picture_vectors, caption_vectors, terms)
    return image_grad, text_grad


def solution(mesh):
    return jax.shard_map(
        on_device,
        mesh=mesh,
        in_specs=(P(("blk", "grp"), None), P(("blk", "grp"), None), P(), P(), P()),
        out_specs=(P(("blk", "grp"), None), P(("blk", "grp"), None)),
        check_vma=False,
    )
```

```python
from functools import partial

import jax
import jax.numpy as jnp
from jax import lax
from jax.experimental import pallas as pl
from jax.experimental.pallas import tpu as pltpu
from jax.sharding import PartitionSpec as P

RING = 4
CORES = 2
TILE = 256
SEND_FLOPS = 10**12
VMEM_BYTES = 24 * 1024 * 1024


def place(x, y, z, core):
    blk = ((x % 2) * RING + y) * CORES + core
    return blk * 8 + z * 2 + x // 2


def sender(move):
    pairs = [
        (place(x, y, z, core), place(*move(x, y, z, core)))
        for x in range(RING)
        for y in range(RING)
        for z in range(RING)
        for core in range(CORES)
    ]
    return lambda value: lax.ppermute(value, ("blk", "grp"), pairs)


def ring(steps):
    return sender(
        lambda x, y, z, c: (x, y, (z + steps) % RING, c) if c else (x, (y + steps) % RING, z, c)
    )


to_core = sender(lambda x, y, z, c: (x, y, z, 1 - c))
cross = sender(lambda x, y, z, c: (3 - x if c else x ^ 1, y, z, c))
up, down = ring(1), ring(RING - 1)


def call(name, body, out_shape, operands, flops, scalars=(), after=(), scratch=()):
    moved = sum(2 * value.size for value in operands) + sum(2 * shape.size for shape in out_shape)
    out = pl.pallas_call(
        lambda *refs: body(*refs[len(after) :]),
        name=name,
        out_shape=out_shape,
        in_specs=[pl.BlockSpec(memory_space=pl.ANY)] * len(after)
        + [pl.BlockSpec(memory_space=pltpu.SMEM)] * len(scalars)
        + [pl.BlockSpec(memory_space=pltpu.VMEM)] * len(operands),
        scratch_shapes=list(scratch),
        compiler_params=pltpu.CompilerParams(vmem_limit_bytes=VMEM_BYTES),
        cost_estimate=pl.CostEstimate(flops=flops // 64, bytes_accessed=moved // 64, transcendentals=0),
    )(*after, *scalars, *operands)
    return list(out)


def array(rows, columns):
    return jax.ShapeDtypeStruct((rows, columns), jnp.bfloat16)


def total_of(terms):
    total = terms[0].astype(jnp.float32)
    for term in terms[1:]:
        total = total + term.astype(jnp.float32)
    return total


def add(*terms, flops=0, after=()):
    def body(*refs):
        refs[-1][...] = total_of([ref[...] for ref in refs[:-1]]).astype(jnp.bfloat16)

    return call("add", body, [array(*terms[0].shape)], terms, flops, after=after)[0]


def unit_of(values):
    inverse = lax.rsqrt(jnp.sum(values * values, axis=1, keepdims=True) + 1e-06)
    return values * inverse, inverse


def unit_halves(core, parameters, batch_total, picture, caption):
    def body(core, warmth, score_offset, multiplier, picture, caption, keep, give, constants):
        scale = jnp.exp(jnp.full((1, TILE), warmth[0], jnp.float32))
        constants[0:1, :] = 0.5 * scale
        constants[1:2, :] = jnp.full((1, TILE), 0.5 * score_offset[0], jnp.float32)
        constants[2:3, :] = 0.5 * (multiplier[0] / batch_total * scale)

        def fill(carried, handed):
            keep[...] = unit_of(carried[...].astype(jnp.float32))[0].astype(jnp.bfloat16)
            give[...] = unit_of(handed[...].astype(jnp.float32))[0].astype(jnp.bfloat16)

        @pl.when(core[0] == 0)
        def _():
            fill(caption, picture)

        @pl.when(core[0] != 0)
        def _():
            fill(picture, caption)

    shapes = [array(*picture.shape)] * 2 + [jax.ShapeDtypeStruct((8, TILE), jnp.float32)]
    return call("units", body, shapes, [picture, caption], 6 * picture.size, [core, *parameters])


def pack(*blocks):
    rows, feature = blocks[0].shape

    def body(*refs):
        for at, ref in enumerate(refs[:-1]):
            refs[-1][pl.ds(at * rows, rows), :] = ref[...]

    return call("pack", body, [array(len(blocks) * rows, feature)], blocks, rows * feature)[0]


def stacked(refs):
    return jnp.concatenate([ref[...] for ref in refs], axis=0)


def sums(name, constants, left, right, held=None, own=False, rows_out=None, after=()):
    feature = left[0].shape[1]
    count, others = sum(ref.shape[0] for ref in left), sum(ref.shape[0] for ref in right)
    blocks = 1 if rows_out is None else count // rows_out

    def body(constants, *refs):
        left_refs, right_refs = refs[: len(left)], refs[len(left) :][: len(right)]
        refs = refs[len(left) + len(right) :]
        out, grads = refs[-1 - blocks : -1], refs[-1]
        slope, shift, factor = constants[0:1, :], constants[1:2, :], constants[2:3, :]
        tiles = [
            (ref, first)
            for ref, block in zip(right_refs, right)
            for first in range(0, block.shape[0], TILE)
        ]

        def scores(tile):
            ref, first = tile
            return lax.dot_general(
                stacked(left_refs),
                ref[pl.ds(first, TILE), :],
                (((1,), (1,)), ((), ())),
                preferred_element_type=jnp.float32,
            )

        upcoming = scores(tiles[0])
        for index in range(len(tiles)):
            current = upcoming
            if index + 1 < len(tiles):
                upcoming = scores(tiles[index + 1])
            bent = jnp.tanh(current * slope + shift) * factor
            offset = factor
            if own and index == 0:
                row = lax.broadcasted_iota(jnp.int32, bent.shape, 0)
                column = lax.broadcasted_iota(jnp.int32, bent.shape, 1)
                half = TILE // 2
                partner = jnp.where(row < half, row + half, row - half)
                paired = jnp.logical_and(column == partner, row < TILE)
                offset = jnp.where(paired, -factor, factor)
            grads[:, pl.ds(index * TILE, TILE)] = (bent + offset).astype(jnp.bfloat16)
        total = jnp.dot(grads[...], stacked(right_refs), preferred_element_type=jnp.float32)
        if held is not None:
            total = total + refs[0][...]
        if rows_out is None:
            out[0][...] = total
        else:
            for at, ref in enumerate(out):
                ref[...] = total[at * rows_out : (at + 1) * rows_out].astype(jnp.bfloat16)

    shapes = (
        [jax.ShapeDtypeStruct((count, feature), jnp.float32)]
        if rows_out is None
        else [array(rows_out, feature)] * blocks
    )
    return call(
        name,
        body,
        shapes,
        [constants, *left, *right] + ([] if held is None else [held]),
        4 * count * others * feature,
        (),
        after,
        [pltpu.VMEM((count, others), jnp.bfloat16)],
    )


def add_half(whole, part, half, flops=0, after=()):
    rows = part.shape[0]

    def body(whole, part, out):
        out[pl.ds((1 - half) * rows, rows), :] = whole[pl.ds((1 - half) * rows, rows), :]
        here = pl.ds(half * rows, rows)
        out[here, :] = total_of([whole[here, :], part[...]]).astype(jnp.bfloat16)

    return call("add_half", body, [array(*whole.shape)], [whole, part], flops, after=after)[0]


def through_norms(core, picture, caption, terms):
    rows, feature = picture.shape

    def give_body(*refs):
        total = total_of([ref[pl.ds(rows, rows), :] for ref in refs[:-1]])
        refs[-1][...] = total.astype(jnp.bfloat16)

    got = to_core(call("give", give_body, [array(rows, feature)], terms, 4 * rows * feature)[0])

    def gradient(raw, direct):
        unit, inverse = unit_of(raw[...].astype(jnp.float32))
        along = jnp.sum(unit * direct, axis=1, keepdims=True)
        return (inverse * (direct - unit * along)).astype(jnp.bfloat16)

    def carried_body(core, picture, caption, *refs):
        direct = total_of([ref[pl.ds(0, rows), :] for ref in refs[:-1]])

        @pl.when(core[0] == 0)
        def _():
            refs[-1][...] = gradient(caption, direct)

        @pl.when(core[0] != 0)
        def _():
            refs[-1][...] = gradient(picture, direct)

    carried = call(
        "carried",
        carried_body,
        [array(rows, feature)],
        [picture, caption, *terms],
        10 * rows * feature,
        [core],
    )[0]

    def body(core, picture, caption, got, carried, image_out, text_out, other, sems):
        def finish(raw, carried_out, other_out):
            carried_copy = pltpu.make_async_copy(carried, carried_out, sems.at[0])
            carried_copy.start()
            other[...] = gradient(raw, got[...].astype(jnp.float32))
            other_copy = pltpu.make_async_copy(other, other_out, sems.at[1])
            other_copy.start()
            carried_copy.wait()
            other_copy.wait()

        @pl.when(core[0] == 0)
        def _():
            finish(picture, text_out, image_out)

        @pl.when(core[0] != 0)
        def _():
            finish(caption, image_out, text_out)

    return pl.pallas_call(
        body,
        name="final",
        out_shape=[array(rows, feature)] * 2,
        in_specs=[pl.BlockSpec(memory_space=pltpu.SMEM)]
        + [pl.BlockSpec(memory_space=pltpu.VMEM)] * 4,
        out_specs=[pl.BlockSpec(memory_space=pl.ANY)] * 2,
        scratch_shapes=[
            pltpu.VMEM((rows, feature), jnp.bfloat16),
            pltpu.SemaphoreType.DMA((2,)),
        ],
        compiler_params=pltpu.CompilerParams(vmem_limit_bytes=VMEM_BYTES),
    )(core, picture, caption, got, carried)


def on_device(
    picture_vectors, caption_vectors, ln_inverse_warmth, score_offset, objective_multiplier
):
    batch_total = picture_vectors.shape[0] * lax.axis_size(("blk", "grp"))
    parameters = [
        value.reshape(1) for value in (ln_inverse_warmth, score_offset, objective_multiplier)
    ]
    core = (lax.axis_index("blk") & (CORES - 1)).reshape(1)
    rows = picture_vectors.shape[0]
    keep, give, constants = unit_halves(
        core, parameters, batch_total, picture_vectors, caption_vectors
    )
    own = jnp.concatenate([keep, to_core(give)], axis=0)
    partner, below, above = cross(own), up(own), down(own)
    partner_above, partner_below, far = cross(above), up(partner), down(above)
    near = [own, partner, above, below]
    near_other = [to_core(block) for block in near]
    near_held = sums("near", constants, near, near_other, own=True)[0]
    partner_below, near_held = lax.optimization_barrier((partner_below, near_held))
    far, near_held = lax.optimization_barrier((far, near_held))
    last = cross(far[:rows]), up(partner_below[rows:])
    middle = [partner_above, partner_below, far]
    middle_other = [to_core(block) for block in middle]
    middle_held = sums("middle", constants, middle, near_other)[0]
    *last, middle_held = lax.optimization_barrier((*last, middle_held))
    last = pack(*last)
    last_other = to_core(last)
    last_held = sums("last", constants, [last], [*near_other, *middle_other])[0]

    last_0, last_1 = sums("last_rest", constants, [last], [last_other], last_held, rows_out=rows)
    to_far, to_below = cross(last_0), down(last_1)
    rest = [*middle_other, last_other]
    partner_above, partner_below, far = sums(
        "middle_rest", constants, middle, rest, middle_held, rows_out=2 * rows, after=[last_0]
    )
    partner_below = add_half(partner_below, to_below, 1, flops=SEND_FLOPS)
    far = add_half(far, to_far, 0, flops=SEND_FLOPS, after=[partner_below])
    to_above, to_partner, to_above_too = up(far), down(partner_below), cross(partner_above)
    own, partner, above, below = sums(
        "near_rest",
        constants,
        near,
        rest,
        near_held,
        rows_out=2 * rows,
        after=[far, partner_below],
    )
    above = add(add(above, to_above_too, flops=SEND_FLOPS), to_above)
    partner = add(partner, to_partner)
    terms = [own, up(above), down(below), cross(partner)]
    image_grad, text_grad = through_norms(core, picture_vectors, caption_vectors, terms)
    return image_grad, text_grad


def solution(mesh):
    return jax.shard_map(
        on_device,
        mesh=mesh,
        in_specs=(P(("blk", "grp"), None), P(("blk", "grp"), None), P(), P(), P()),
        out_specs=(P(("blk", "grp"), None), P(("blk", "grp"), None)),
        check_vma=False,
    )
```
